512 devices in a mesh: section: 8 (over x, core), store: 64 (over y, z).
Axes of the slice: x: 4, y: 4, z: 16, core: 2. Of those that a mesh axis runs over, the one named last changes fastest.
Arguments:
- hidden_in: bfloat16 [8, 1536, 3584], P('section', 'store'), may hold values from -6 to 6
- incoming: bfloat16 [1536, 3584], P('store'), may hold values from -6 to 6
- routes: int32 [2, 8, 1536, 2], P(None, 'section', 'store'), may hold values from 0 to 7, all different within a row; in each aligned block of 24 rows (0 to 23, 24 to 47, ..., all dimensions but the last counted through in order) at most 8 rows name the same one
- gates: float32 [2, 8, 1536, 2], P(None, 'section', 'store'), may hold values from 0.2 to 2
- norm_gain: float32 [8, 3584], P('section'), may hold values from 0.1 to 1.9
- w_gate: bfloat16 [8, 3584, 8192], P('section', None, 'store'), may hold values from -0.09375 to 0.09375
- w_up: bfloat16 [8, 3584, 8192], P('section', None, 'store'), may hold values from -0.09375 to 0.09375
- w_down: bfloat16 [8, 8192, 3584], P('section', 'store'), may hold values from -0.1875 to 0.1875
Outputs:
- after_first: bfloat16 [8, 1536, 3584], P('section', 'store')
- after_second: bfloat16 [8, 1536, 3584], P('section', 'store')
The draws below stay inside these ranges and needn't reach their ends.
Inputs may be any that keep to these rules, and one draw needn't show every extreme that they name: `routes`: each row names 2 different experts; among the rows of one device (aligned blocks of 24 rows) no expert is named more than 8 times, a bound that some block reaches.
All inputs are finite; a program needn't handle non-finite values.
Results may differ from the reference program's by a relative error of at most 0.018.
Values may be sent and summed in bfloat16 or wider, within the bound.
No kernel may reach another device: no remote copies, remote signals or barrier semaphores. Data moves between devices by JAX's collectives and lax.ppermute only.
A program may use at most 64 MiB of HBM per device.

```python
import math
from functools import partial
import jax
import jax.numpy as jnp
import numpy as np
from jax import lax

D = 3584
FF = 1024
TOPK = 2
TICKS = 2
ROWS_DEV = 24
HS = 8
HD = 128
SECTIONS = 8
EXPERTS = 8
TOKENS = 1536
CAP = 8
N_STORE = 64


def block_levels(rng, shape, cuts, least, high):
    level, own = 1.0, jax.random.fold_in(rng, 6)
    for dim, blocks in cuts:
        heights = jnp.exp(jax.random.uniform(jax.random.fold_in(own, dim), (blocks,), jnp.float32, least / len(cuts), high / len(cuts)))
        level = level * jnp.repeat(heights, shape[dim] // blocks).reshape([-1 if axis == dim else 1 for axis in range(len(shape))])
    return level


def routed_block(stream_key, own, number, rows, number_of, top, limit, skew):
    ranking = jax.random.permutation(stream_key, number_of)
    heavy_load, common = portions_of(number_of, rows * top, limit, skew, True), portions_of(number_of, rows * top, limit, skew, False)
    places = jnp.arange(number_of)

    def named(lengths, rotation):
        used = int((lengths > 0).sum())
        fixed = max(1, used // 4)
        passed = fixed + (places - fixed + rotation * (used - fixed)) % max(1, number_of - fixed)
        return jnp.zeros((number_of,), jnp.int32).at[ranking[jnp.where(places < fixed, places, passed)]].set(jnp.asarray(lengths, jnp.int32))

    lengths = jnp.where(number % 4 == 0, named(heavy_load, number // 4), named(common, number - number // 4 - 1))
    mixed = jax.random.permutation(jax.random.fold_in(own, 3), number_of)
    giver, sink = mixed[0:number_of // 2 * 2:2], mixed[1:number_of // 2 * 2:2]
    margin = jnp.minimum(lengths[giver] - 1, limit - lengths[sink]) // 2
    margin = jnp.where((giver == ranking[0]) | (sink == ranking[0]) | (lengths[sink] == 0), 0, jnp.maximum(margin, 0))
    passed = jax.random.randint(jax.random.fold_in(own, 4), (number_of // 2,), 0, 1 << 20) % (margin + 1)
    lengths = lengths.at[giver].add(-passed).at[sink].add(passed)
    items = jnp.searchsorted(jnp.cumsum(lengths), jnp.arange(rows * top), side="right").astype(jnp.int32)
    grid = items.reshape(top, rows).T
    grid = grid[jax.random.permutation(jax.random.fold_in(own, 1), rows)]
    rotation = jax.random.randint(jax.random.fold_in(own, 2), (rows, 1), 0, top)
    return jnp.take_along_axis(grid, (jnp.arange(top)[None, :] + rotation) % top, axis=1)


def portions_of(number_of, total, limit, skew, full):
    portions = [(1 << 20) // math.isqrt(standing ** skew) + 1 for standing in range(1, number_of + 1)]
    largest = limit if full else min(limit, max(-(-total // number_of), total * portions[0] // sum(portions)))
    least = 1 if total - largest >= number_of - 1 else 0
    holding, rest = [largest] + [least] * (number_of - 1), total - largest - least * (number_of - 1)
    while rest > 0:
        free = [i for i in range(1, number_of) if holding[i] < largest] or [i for i in range(1, number_of) if holding[i] < limit]
        whole, budget = sum([portions[i] for i in free]), rest
        for i in free:
            more = min(limit - holding[i], max(1, budget * portions[i] // whole), rest)
            holding[i] = holding[i] + more
            rest = rest - more
    return np.array(holding)


def gaussian(stream_key, shape, deviation, bound, cuts=(), held_as=jnp.bfloat16):
    entries = deviation * jax.random.normal(stream_key, shape, jnp.float32)
    if cuts:
        entries = entries * block_levels(stream_key, shape, cuts, -0.22, 0.18)
    return jnp.clip(entries, -bound, bound).astype(held_as)


def setup_inputs(seed: int = 0) -> dict:
    arg_keys = jax.random.split(jax.random.key(seed), 9)
    hidden_in = gaussian(arg_keys[0], (SECTIONS, TOKENS, D), 1.0, 6.0, ((0, 8), (1, 64)))
    incoming = gaussian(arg_keys[1], (TOKENS, D), 1.0, 6.0, ((0, 64),))
    routes_keys = jax.random.split(jax.random.fold_in(arg_keys[2], 1), TICKS * SECTIONS * TOKENS // ROWS_DEV)
    routes_turns = jax.random.permutation(jax.random.fold_in(arg_keys[2], 3), TICKS * SECTIONS * TOKENS // ROWS_DEV)
    routes = jax.vmap(lambda own, number: routed_block(jax.random.fold_in(arg_keys[2], 2), own, number, ROWS_DEV, EXPERTS, TOPK, CAP, 2))(routes_keys, routes_turns).reshape((TICKS, SECTIONS, TOKENS, TOPK))
    gates = jnp.clip(jnp.exp(math.log(2.0) - 2.3025851 * jax.random.uniform(arg_keys[3], (TICKS, SECTIONS, TOKENS, TOPK), jnp.float32) ** block_levels(arg_keys[3], (TICKS, SECTIONS, TOKENS, TOPK), ((1, 8), (2, 64)), -0.2, 0.2)), 0.2, 2.0)
    norm_gain = jnp.clip(1.0 + 0.18 * jax.random.normal(arg_keys[4], (SECTIONS, D), jnp.float32), 0.1, 1.9)
    w_gate = gaussian(arg_keys[5], (SECTIONS, D, EXPERTS * FF), D ** -0.5, 0.09375, ((0, 8), (2, 64)))
    w_up = gaussian(arg_keys[6], (SECTIONS, D, EXPERTS * FF), D ** -0.5, 0.09375, ((0, 8), (2, 64)))
    w_down = gaussian(arg_keys[7], (SECTIONS, EXPERTS * FF, D), FF ** -0.5, 0.1875, ((0, 8), (1, 64)))
    return {"hidden_in": hidden_in, "incoming": incoming, "routes": routes, "gates": gates, "norm_gain": norm_gain, "w_gate": w_gate, "w_up": w_up, "w_down": w_down}


HIGH = lax.Precision.HIGHEST

def norm_rows(acts, gain):
    values = acts.astype(jnp.float32)
    scale = lax.rsqrt(lax.optimization_barrier(jnp.mean(values * values, axis=-1, keepdims=True)) + 1e-06)
    return ((values * scale * gain).astype(jnp.bfloat16), values)

def slot_tables(picks, weights, experts, capacity):
    rows, topk = picks.shape
    flat = picks.reshape(-1)
    onehot = (flat[:, None] == jnp.arange(experts, dtype=jnp.int32)[None, :]).astype(jnp.int32)
    before = jnp.cumsum(onehot, axis=0) - onehot
    position = lax.optimization_barrier(jnp.sum(before * onehot, axis=1))
    slot = flat * capacity + position
    chosen = (slot[:, None] == jnp.arange(experts * capacity, dtype=jnp.int32)[None, :]).astype(jnp.float32)
    chosen = chosen.reshape(rows, topk, experts * capacity)
    dispatch = lax.optimization_barrier(jnp.sum(chosen, axis=1))
    combine = lax.optimization_barrier(jnp.sum(chosen * weights[:, :, None], axis=1))
    return (dispatch, combine)

def one_expert(operands):
    rows, gate_w, up_w, down_w = operands
    rows_f = rows.astype(jnp.float32)
    gate = jnp.dot(rows_f, gate_w.astype(jnp.float32), precision=HIGH)
    upper = jnp.dot(rows_f, up_w.astype(jnp.float32), precision=HIGH)
    hidden = (jax.nn.silu(gate) * upper).astype(jnp.bfloat16)
    pieces = jnp.einsum('rsh,shd->srd', hidden.reshape(rows.shape[0], HS, HD).astype(jnp.float32), down_w.reshape(HS, HD, D).astype(jnp.float32), precision=HIGH)
    return lax.optimization_barrier(jnp.sum(pieces.astype(jnp.bfloat16).astype(jnp.float32), axis=0))

def layer(acts, picks, weights, gain, gate_w, up_w, down_w):
    normed, values = norm_rows(acts, gain)
    blocks = normed.reshape(N_STORE, ROWS_DEV, D)
    dispatch, combine = jax.vmap(partial(slot_tables, experts=EXPERTS, capacity=CAP))(picks.reshape(N_STORE, ROWS_DEV, TOPK), weights.reshape(N_STORE, ROWS_DEV, TOPK))
    sent = jnp.einsum('brs,brd->bsd', dispatch, blocks.astype(jnp.float32), precision=HIGH).astype(jnp.bfloat16)
    sent = sent.reshape(N_STORE, EXPERTS, CAP, D).transpose(1, 0, 2, 3).reshape(EXPERTS, N_STORE * CAP, D)
    gate_e = gate_w.reshape(D, EXPERTS, FF).transpose(1, 0, 2)
    up_e = up_w.reshape(D, EXPERTS, FF).transpose(1, 0, 2)
    down_e = down_w.reshape(EXPERTS, FF, D)
    outputs = lax.map(one_expert, (sent, gate_e, up_e, down_e))
    outputs = outputs.reshape(EXPERTS, N_STORE, CAP, D).transpose(1, 0, 2, 3).reshape(N_STORE, EXPERTS * CAP, D)
    mixed = jnp.einsum('brs,bsd->brd', combine, outputs, precision=HIGH).reshape(TOKENS, D)
    return (values + mixed).astype(jnp.bfloat16)

def reference(hidden_in, incoming, routes, gates, norm_gain, w_gate, w_up, w_down):
    first = []
    for section in range(SECTIONS):
        first.append(layer(hidden_in[section], routes[0, section], gates[0, section], norm_gain[section], w_gate[section], w_up[section], w_down[section]))
    second = []
    for section in range(SECTIONS):
        entry = incoming if section == 0 else first[section - 1]
        second.append(layer(entry, routes[1, section], gates[1, section], norm_gain[section], w_gate[section], w_up[section], w_down[section]))
    return (jnp.stack(first), jnp.stack(second))
```

```python
import jax
import jax.numpy as jnp
from jax import lax
from jax.sharding import Mesh, PartitionSpec as P

TOPK = 2
HS = 8
QUARTERS = 4


HIGH = lax.Precision.HIGHEST
STORE = ("y", "q", "b")


def shifted(shard, axis, by):
    peers = lax.axis_size(axis)
    pairs = [(i, i + by) for i in range(peers) if 0 <= i + by < peers]
    return lax.ppermute(shard, axis, pairs)


def swap(blocks, axis):
    return lax.all_to_all(blocks, axis, split_axis=0, concat_axis=0, tiled=True)


def norm_rows(acts, gain):
    values = acts.astype(jnp.float32)
    scale = lax.rsqrt(jnp.mean(values * values, axis=-1, keepdims=True) + 1e-06)
    return ((values * scale * gain).astype(jnp.bfloat16), values)


def slot_tables(picks, weights, experts, capacity):
    rows, topk = picks.shape
    flat = picks.reshape(-1)
    onehot = (flat[:, None] == jnp.arange(experts, dtype=jnp.int32)[None, :]).astype(jnp.int32)
    before = jnp.cumsum(onehot, axis=0) - onehot
    position = jnp.sum(before * onehot, axis=1)
    slot = flat * capacity + position
    chosen = (slot[:, None] == jnp.arange(experts * capacity, dtype=jnp.int32)[None, :]).astype(
        jnp.float32
    )
    chosen = chosen.reshape(rows, topk, experts * capacity)
    dispatch = jnp.sum(chosen, axis=1)
    combine = jnp.sum(chosen * weights[:, :, None], axis=1)
    return (dispatch, combine)


def layer(acts, tables, gain, in_w, out_w):
    dispatch, combine = tables
    rows, width = acts.shape
    n_store = lax.axis_size(STORE)
    experts = n_store // HS
    capacity = dispatch.shape[1] // experts
    part = width // QUARTERS
    halves = HS // QUARTERS
    normed, values = norm_rows(acts, gain)
    packed = jnp.einsum(
        "rep,rbf->ebpf",
        dispatch.astype(jnp.bfloat16).reshape(rows, experts, capacity),
        normed.reshape(rows, QUARTERS, part),
        preferred_element_type=jnp.float32,
    ).astype(jnp.bfloat16)
    outgoing = jnp.broadcast_to(
        packed[:, None], (experts, halves, QUARTERS, capacity, part)
    ).reshape(n_store, capacity, part)
    received = swap(outgoing, STORE).reshape(-1, part)
    partial_in = jnp.einsum(
        "rf,bfh->brh", received, in_w, preferred_element_type=jnp.float32
    ).astype(jnp.bfloat16)
    sums = jnp.sum(swap(partial_in, "b").astype(jnp.float32), axis=0)
    mine = sums.shape[1] // 2
    hidden = (jax.nn.silu(sums[:, :mine]) * sums[:, mine:]).astype(jnp.bfloat16)
    hidden = lax.all_gather(hidden, "b", axis=0)
    partial_out = jnp.einsum(
        "brh,bhf->rf", hidden, out_w, preferred_element_type=jnp.float32
    ).astype(jnp.bfloat16)
    returned = swap(partial_out.reshape(n_store, capacity, part), STORE)
    returned = returned.reshape(experts, halves, QUARTERS, capacity, part)
    summed = jnp.sum(returned.astype(jnp.float32), axis=1)
    mixed = jnp.einsum(
        "rep,ebpf->rbf", combine.reshape(rows, experts, capacity), summed, precision=HIGH
    ).reshape(rows, width)
    return (values + mixed).astype(jnp.bfloat16)


def on_device(hidden_in, incoming, routes, gates, norm_gain, w_gate, w_up, w_down):
    section_place = lax.axis_index("section")
    rows, width = incoming.shape
    n_store = lax.axis_size(STORE)
    experts = n_store // HS
    capacity = HS * ((rows * TOPK + experts * HS - 1) // (experts * HS))
    part = width // QUARTERS
    in_w = jnp.concatenate([w_gate[0], w_up[0]], axis=1).reshape(QUARTERS, part, -1)
    in_w = swap(in_w, "b")
    out_w = w_down[0].reshape(-1, QUARTERS, part).transpose(1, 0, 2)
    out_w = swap(out_w, "b")
    tables = [slot_tables(routes[t, 0], gates[t, 0], experts, capacity) for t in range(2)]
    first = layer(hidden_in[0], tables[0], norm_gain[0], in_w, out_w)
    handed = shifted(first, "section", 1)
    entry = jnp.where(section_place == 0, incoming, handed)
    second = layer(entry, tables[1], norm_gain[0], in_w, out_w)
    return (first[None], second[None])


def solution(mesh):
    sections, stores = mesh.devices.shape
    fine = Mesh(
        mesh.devices.reshape(sections, 4, stores // (4 * QUARTERS), QUARTERS),
        ("section",) + STORE,
    )
    placed = (
        P("section", STORE, None),
        P(STORE, None),
        P(None, "section", STORE, None),
        P(None, "section", STORE, None),
        P("section", None),
        P("section", None, STORE),
        P("section", None, STORE),
        P("section", STORE, None),
    )
    return jax.shard_map(
        on_device,
        mesh=fine,
        in_specs=placed,
        out_specs=(P("section", STORE, None), P("section", STORE, None)),
        check_vma=False,
    )
```

```python
import jax
import jax.numpy as jnp
from jax import lax
from jax.sharding import Mesh, PartitionSpec as P

TOPK = 2
HS = 8
QUARTERS = 4


HIGH = lax.Precision.HIGHEST
RING = ("q", "b")
STORE = ("y",) + RING


def shifted(shard, axis, by):
    peers = lax.axis_size(axis)
    pairs = [(i, i + by) for i in range(peers) if 0 <= i + by < peers]
    return lax.ppermute(shard, axis, pairs)


def fetched(shard, axis, ahead):
    peers = lax.axis_size(axis)
    return lax.ppermute(shard, axis, [((i + ahead) % peers, i) for i in range(peers)])


def swap(blocks, axis):
    return lax.all_to_all(blocks, axis, split_axis=0, concat_axis=0, tiled=True)


def norm_rows(acts, gain):
    values = acts.astype(jnp.float32)
    scale = lax.rsqrt(jnp.mean(values * values, axis=-1, keepdims=True) + 1e-06)
    return ((values * scale * gain).astype(jnp.bfloat16), values)


def row_tables(picks, weights, wanted, capacity):
    blocks, rows, _ = picks.shape
    hit = (picks[None] == wanted[:, None, None, None]).astype(jnp.float32)
    gate = jnp.sum(hit * weights[None], axis=-1)
    hit = jnp.sum(hit, axis=-1)
    earlier = jnp.triu(jnp.ones((rows, rows), jnp.float32), 1)
    position = jnp.einsum("dst,tu->dsu", hit, earlier, precision=HIGH).astype(jnp.int32)
    place = jnp.arange(blocks, dtype=jnp.int32)[None, :, None] * capacity + position
    place = jnp.where(hit > 0, place, -1).reshape(wanted.shape[0], blocks * rows)
    slots = jnp.arange(blocks * capacity, dtype=jnp.int32)
    pack = (slots[None, :, None] == place[:, None, :]).astype(jnp.bfloat16)
    chosen = (place[:, :, None] == slots[None, None, :]).astype(jnp.float32)
    unpack = chosen * gate.reshape(wanted.shape[0], blocks * rows, 1)
    return (pack, unpack)


def layer(acts, tables, gain, in_w, out_w):
    pack, unpack = tables
    rows, width = acts.shape
    part = width // QUARTERS
    normed, values = norm_rows(acts, gain)
    tokens = lax.all_gather(normed, RING, tiled=True)
    packed = []
    for ahead in range(QUARTERS):
        inner = jnp.dot(tokens, in_w[ahead], preferred_element_type=jnp.float32)
        mine = inner.shape[1] // 2
        hidden = (jax.nn.silu(inner[:, :mine]) * inner[:, mine:]).astype(jnp.bfloat16)
        packed.append(
            jnp.dot(pack[ahead], hidden, preferred_element_type=jnp.float32).astype(jnp.bfloat16)
        )
    hidden = lax.all_gather(jnp.stack(packed), "b", axis=0)
    mixed = 0.0
    for ahead in range(QUARTERS):
        units = hidden[:, ahead].transpose(1, 0, 2).reshape(hidden.shape[2], -1)
        out = jnp.dot(units, out_w[ahead], preferred_element_type=jnp.float32)
        mixed = mixed + jnp.dot(unpack[ahead], out, precision=HIGH)
    returned = swap(mixed.astype(jnp.bfloat16).reshape(-1, rows, part), RING)
    returned = returned.reshape(-1, QUARTERS, rows, part).astype(jnp.float32)
    summed = jnp.sum(returned, axis=0).transpose(1, 0, 2).reshape(rows, width)
    return (values + summed).astype(jnp.bfloat16)


def on_device(hidden_in, incoming, routes, gates, norm_gain, w_gate, w_up, w_down):
    section_place = lax.axis_index("section")
    rows, width = incoming.shape
    n_store = lax.axis_size(STORE)
    experts = n_store // HS
    capacity = HS * ((rows * TOPK + experts * HS - 1) // (experts * HS))
    part = width // QUARTERS
    in_w = jnp.concatenate([w_gate[0], w_up[0]], axis=1)
    out_w = w_down[0].reshape(-1, QUARTERS, part).transpose(1, 0, 2)
    out_w = swap(out_w, "b").reshape(-1, part)
    in_w = [in_w] + [fetched(in_w, "y", ahead) for ahead in (1, 2, 3)]
    out_w = [out_w] + [fetched(out_w, "y", ahead) for ahead in (1, 2, 3)]

    ring_place = lax.axis_index(RING)
    per_row = lax.axis_size(RING) // HS
    y_place = (lax.axis_index("y") + jnp.arange(QUARTERS, dtype=jnp.int32)) % QUARTERS
    wanted = y_place * per_row + ring_place // HS
    facts = jnp.stack([routes[:, 0].astype(jnp.float32), gates[:, 0]])
    facts = lax.all_gather(facts.reshape(1, -1), RING, tiled=True)
    facts = facts.reshape(-1, 2, 2, rows, TOPK)
    tables = [
        row_tables(facts[:, 0, t].astype(jnp.int32), facts[:, 1, t], wanted, capacity)
        for t in range(2)
    ]
    first = layer(hidden_in[0], tables[0], norm_gain[0], in_w, out_w)
    handed = shifted(first, "section", 1)
    entry = jnp.where(section_place == 0, incoming, handed)
    second = layer(entry, tables[1], norm_gain[0], in_w, out_w)
    return (first[None], second[None])


def solution(mesh):
    sections, stores = mesh.devices.shape
    fine = Mesh(
        mesh.devices.reshape(sections, 4, stores // (4 * QUARTERS), QUARTERS),
        ("section",) + STORE,
    )
    placed = (
        P("section", STORE, None),
        P(STORE, None),
        P(None, "section", STORE, None),
        P(None, "section", STORE, None),
        P("section", None),
        P("section", None, STORE),
        P("section", None, STORE),
        P("section", STORE, None),
    )
    return jax.shard_map(
        on_device,
        mesh=fine,
        in_specs=placed,
        out_specs=(P("section", STORE, None), P("section", STORE, None)),
        check_vma=False,
    )
```

```python
import functools

import jax
import jax.numpy as jnp
from jax import lax
from jax.experimental import pallas as pl
from jax.experimental.pallas import tpu as pltpu
from jax.sharding import Mesh, PartitionSpec as P

TOPK = 2
HS = 8
QUARTERS = 4


HIGH = lax.Precision.HIGHEST
RING = ("q", "b")
STORE = ("y",) + RING
MIB = 1 << 20


def shifted(shard, axis, by):
    peers = lax.axis_size(axis)
    pairs = [(i, i + by) for i in range(peers) if 0 <= i + by < peers]
    return lax.ppermute(shard, axis, pairs)


def fetched(shard, axis, ahead):
    peers = lax.axis_size(axis)
    return lax.ppermute(shard, axis, [((i + ahead) % peers, i) for i in range(peers)])


def swap(blocks, axis):
    return lax.all_to_all(blocks, axis, split_axis=0, concat_axis=0, tiled=True)


def whole_row(shard):
    half = shard.shape[0] // 2
    after = fetched(shard, "y", 1)
    before = fetched(shard, "y", 3)
    far_top = fetched(after[:half], "y", 1)
    far_bottom = fetched(before[half:], "y", 3)
    return (shard, after, far_top, far_bottom, before)


def loads(pieces, buffer, sems):
    own, after, far_top, far_bottom, before = pieces
    half = far_top.shape[0]
    return [
        [pltpu.make_async_copy(own, buffer.at[0], sems.at[0])],
        [pltpu.make_async_copy(after, buffer.at[1], sems.at[1])],
        [
            pltpu.make_async_copy(far_top, buffer.at[2, pl.ds(0, half)], sems.at[2]),
            pltpu.make_async_copy(far_bottom, buffer.at[2, pl.ds(half, half)], sems.at[3]),
        ],
        [pltpu.make_async_copy(before, buffer.at[3], sems.at[4])],
    ]


def entry_kernel(first_ref, fed_ref, handed_ref, gain_ref, entry_ref, normed_ref):
    acts = jnp.where(first_ref[0] == 1, fed_ref[...], handed_ref[...])
    entry_ref[...] = acts
    values = acts.astype(jnp.float32)
    scale = lax.rsqrt(jnp.mean(values * values, axis=-1, keepdims=True) + 1e-06)
    normed_ref[...] = (values * scale * gain_ref[...]).astype(jnp.bfloat16)


def enter(is_first, fed, handed, gain):
    vmem = pl.BlockSpec(memory_space=pltpu.VMEM)
    return pl.pallas_call(
        entry_kernel,
        out_shape=(jax.ShapeDtypeStruct(fed.shape, fed.dtype),) * 2,
        in_specs=[pl.BlockSpec(memory_space=pltpu.SMEM), vmem, vmem, vmem],
        out_specs=(vmem, vmem),
        cost_estimate=pl.CostEstimate(flops=6 * fed.size, bytes_accessed=8 * fed.size, transcendentals=0),
        name="enter",
    )(is_first, fed, handed, gain)


def up_kernel(tokens_ref, own, after, far_top, far_bottom, before, place_ref, packed_ref, tokens, weights, sems, token_sem):
    token_copy = pltpu.make_async_copy(tokens_ref, tokens, token_sem)
    token_copy.start()
    copies = loads((own, after, far_top, far_bottom, before), weights, sems)
    for group in copies:
        for copy in group:
            copy.start()
    token_copy.wait()
    rows = tokens.shape[0]
    slots = packed_ref.shape[1]
    for ahead in range(QUARTERS):
        for copy in copies[ahead]:
            copy.wait()
        inner = jnp.dot(tokens[...], weights[ahead], preferred_element_type=jnp.float32)
        mine = inner.shape[1] // 2
        gate = inner[:, :mine]
        hidden = (gate / (1.0 + jnp.exp(-gate)) * inner[:, mine:]).astype(jnp.bfloat16)
        slot = lax.broadcasted_iota(jnp.int32, (slots, rows), 0)
        pack = jnp.where(slot == place_ref[ahead : ahead + 1, :], 1.0, 0.0).astype(jnp.bfloat16)
        packed = jnp.dot(pack, hidden, preferred_element_type=jnp.float32)
        packed_ref[ahead] = packed.astype(jnp.bfloat16)


def expert_up(tokens, in_w, place, slots):
    rows, width = tokens.shape
    units = in_w[0].shape[1]
    any_space = pl.BlockSpec(memory_space=pl.ANY)
    vmem = pl.BlockSpec(memory_space=pltpu.VMEM)
    return pl.pallas_call(
        up_kernel,
        out_shape=jax.ShapeDtypeStruct((QUARTERS, slots, units // 2), jnp.bfloat16),
        in_specs=[any_space] * 6 + [vmem],
        out_specs=vmem,
        scratch_shapes=[
            pltpu.VMEM((rows, width), jnp.bfloat16),
            pltpu.VMEM((QUARTERS, width, units), jnp.bfloat16),
            pltpu.SemaphoreType.DMA((5,)),
            pltpu.SemaphoreType.DMA,
        ],
        compiler_params=pltpu.CompilerParams(vmem_limit_bytes=32 * MIB),
        cost_estimate=pl.CostEstimate(
            flops=2 * QUARTERS * rows * width * units,
            bytes_accessed=2 * width * (rows + QUARTERS * units),
            transcendentals=rows * units * 2,
        ),
        name="expert_up",
    )(tokens, *in_w, place)


def down_kernel(hidden_ref, own, after, far_top, far_bottom, before, place_ref, gate_ref, out_ref, weights, sems):
    copies = loads((own, after, far_top, far_bottom, before), weights, sems)
    for group in copies:
        for copy in group:
            copy.start()
    rows = out_ref.shape[0]
    slots = hidden_ref.shape[2]
    mixed = None
    for ahead in range(QUARTERS):
        for copy in copies[ahead]:
            copy.wait()
        units = jnp.concatenate([hidden_ref[b, ahead] for b in range(QUARTERS)], axis=1)
        out = jnp.dot(units, weights[ahead], preferred_element_type=jnp.float32)
        high = out.astype(jnp.bfloat16)
        low = (out - high.astype(jnp.float32)).astype(jnp.bfloat16)
        slot = lax.broadcasted_iota(jnp.int32, (rows, slots), 1)
        unpack = jnp.where(slot == place_ref[:, ahead : ahead + 1], 1.0, 0.0).astype(jnp.bfloat16)
        placed = jnp.dot(unpack, high, preferred_element_type=jnp.float32)
        placed = placed + jnp.dot(unpack, low, preferred_element_type=jnp.float32)
        placed = placed * gate_ref[:, ahead : ahead + 1]
        mixed = placed if mixed is None else mixed + placed
    out_ref[...] = mixed.astype(jnp.bfloat16)


def expert_down(hidden, out_w, place, gate):
    rows = place.shape[0]
    units, part = out_w[0].shape
    slots = hidden.shape[2]
    any_space = pl.BlockSpec(memory_space=pl.ANY)
    vmem = pl.BlockSpec(memory_space=pltpu.VMEM)
    return pl.pallas_call(
        down_kernel,
        out_shape=jax.ShapeDtypeStruct((rows, part), jnp.bfloat16),
        in_specs=[vmem] + [any_space] * 5 + [vmem] * 2,
        out_specs=vmem,
        scratch_shapes=[
            pltpu.VMEM((QUARTERS, units, part), jnp.bfloat16),
            pltpu.SemaphoreType.DMA((5,)),
        ],
        compiler_params=pltpu.CompilerParams(vmem_limit_bytes=32 * MIB),
        cost_estimate=pl.CostEstimate(
            flops=2 * QUARTERS * slots * part * (units + 2 * rows),
            bytes_accessed=2 * QUARTERS * units * (part + slots),
            transcendentals=0,
        ),
        name="expert_down",
    )(hidden, *out_w, place, gate)


def leave_kernel(entry_ref, returned_ref, out_ref):
    part = returned_ref.shape[2]
    for b in range(QUARTERS):
        columns = pl.ds(b * part, part)
        total = entry_ref[:, columns].astype(jnp.float32)
        for q in range(returned_ref.shape[0] // QUARTERS):
            total = total + returned_ref[q * QUARTERS + b].astype(jnp.float32)
        out_ref[:, columns] = total.astype(jnp.bfloat16)


def leave(entry, returned):
    vmem = pl.BlockSpec(memory_space=pltpu.VMEM)
    return pl.pallas_call(
        leave_kernel,
        out_shape=jax.ShapeDtypeStruct(entry.shape, jnp.bfloat16),
        in_specs=[vmem] * 2,
        out_specs=vmem,
        cost_estimate=pl.CostEstimate(
            flops=returned.size, bytes_accessed=2 * returned.size + 4 * entry.size, transcendentals=0
        ),
        name="leave",
    )(entry, returned)


def row_tables(picks, weights, wanted, capacity):
    blocks, rows, _ = picks.shape
    hit = (picks[None] == wanted[:, None, None, None]).astype(jnp.float32)
    gate = jnp.sum(hit * weights[None], axis=-1)
    hit = jnp.sum(hit, axis=-1)
    earlier = jnp.triu(jnp.ones((rows, rows), jnp.float32), 1)
    position = jnp.einsum("dst,tu->dsu", hit, earlier, precision=HIGH).astype(jnp.int32)
    place = jnp.arange(blocks, dtype=jnp.int32)[None, :, None] * capacity + position
    place = jnp.where(hit > 0, place, -1).reshape(wanted.shape[0], blocks * rows)
    return (place, place.T, gate.reshape(wanted.shape[0], blocks * rows).T)


def layer(entry, normed, tables, in_w, out_w, slots):
    place, place_t, gate_t = tables
    rows, width = entry.shape
    tokens = lax.all_gather(normed, RING, tiled=True)
    hidden = expert_up(tokens, in_w, place, slots)
    hidden = lax.all_gather(hidden, "b", axis=0)
    mixed = expert_down(hidden, out_w, place_t, gate_t)
    returned = swap(mixed.reshape(-1, rows, width // QUARTERS), RING)
    return leave(entry, returned)


def on_device(hidden_in, incoming, routes, gates, norm_gain, w_gate, w_up, w_down):
    section_place = lax.axis_index("section")
    rows, width = incoming.shape
    n_store = lax.axis_size(STORE)
    experts = n_store // HS
    capacity = HS * ((rows * TOPK + experts * HS - 1) // (experts * HS))
    part = width // QUARTERS
    one = jnp.ones((1,), jnp.int32)
    entry, normed = enter(one, hidden_in[0], hidden_in[0], norm_gain)

    in_w = whole_row(jnp.concatenate([w_gate[0], w_up[0]], axis=1))
    out_w = w_down[0].reshape(-1, QUARTERS, part).transpose(1, 0, 2)
    out_w = whole_row(swap(out_w, "b").reshape(-1, part))

    ring = lax.axis_size(RING)
    ring_place = lax.axis_index(RING)
    y_place = (lax.axis_index("y") + jnp.arange(QUARTERS, dtype=jnp.int32)) % QUARTERS
    wanted = y_place * (ring // HS) + ring_place // HS
    facts = jnp.stack([routes[:, 0].astype(jnp.float32), gates[:, 0]])
    facts = swap(jnp.broadcast_to(facts.reshape(1, 1, -1), (ring, 1, facts.size)), RING)
    facts = facts.reshape(ring, 2, 2, rows, TOPK)
    tables = [
        row_tables(facts[:, 0, t].astype(jnp.int32), facts[:, 1, t], wanted, capacity)
        for t in range(2)
    ]
    slots = ring * capacity
    first = layer(entry, normed, tables[0], in_w, out_w, slots)
    handed = shifted(first, "section", 1)
    is_first = (section_place == 0).astype(jnp.int32).reshape(1)
    entry, normed = enter(is_first, incoming, handed, norm_gain)
    second = layer(entry, normed, tables[1], in_w, out_w, slots)
    return (first[None], second[None])


def solution(mesh):
    sections, stores = mesh.devices.shape
    fine = Mesh(
        mesh.devices.reshape(sections, 4, stores // (4 * QUARTERS), QUARTERS),
        ("section",) + STORE,
    )
    placed = (
        P("section", STORE, None),
        P(STORE, None),
        P(None, "section", STORE, None),
        P(None, "section", STORE, None),
        P("section", None),
        P("section", None, STORE),
        P("section", None, STORE),
        P("section", STORE, None),
    )
    return jax.shard_map(
        on_device,
        mesh=fine,
        in_specs=placed,
        out_specs=(P("section", STORE, None), P("section", STORE, None)),
        check_vma=False,
    )
```

```python
import functools

import jax
import jax.numpy as jnp
from jax import lax
from jax.experimental import pallas as pl
from jax.experimental.pallas import tpu as pltpu
from jax.sharding import Mesh, PartitionSpec as P

TOPK = 2
HS = 8
QUARTERS = 4


HIGH = lax.Precision.HIGHEST
RING = ("q", "b")
STORE = ("y",) + RING
MIB = 1 << 20
LANES = 128
SUBLANES = 8


def shifted(shard, axis, by):
    peers = lax.axis_size(axis)
    pairs = [(i, i + by) for i in range(peers) if 0 <= i + by < peers]
    return lax.ppermute(shard, axis, pairs)


def fetched(shard, axis, ahead):
    peers = lax.axis_size(axis)
    return lax.ppermute(shard, axis, [((i + ahead) % peers, i) for i in range(peers)])


def swap(blocks, axis):
    return lax.all_to_all(blocks, axis, split_axis=0, concat_axis=0, tiled=True)


def send_rows(tick, acts, gain_ref, routes_ref, gates_ref, sent_ref, table):
    rows, width = acts.shape
    values = acts.astype(jnp.float32)
    scale = lax.rsqrt(jnp.mean(values * values, axis=-1, keepdims=True) + 1e-06)
    sent_ref[:, :width] = (values * scale * gain_ref[...]).astype(jnp.bfloat16)
    gates = gates_ref[tick]
    high = gates.astype(jnp.bfloat16).astype(jnp.float32)
    middle = (gates - high).astype(jnp.bfloat16).astype(jnp.float32)
    table[...] = jnp.zeros_like(table)
    table[0:2, 0:rows] = routes_ref[tick].astype(jnp.float32)
    table[2:4, 0:rows] = high
    table[4:6, 0:rows] = middle
    table[6:8, 0:rows] = gates - high - middle
    sent_ref[:, width:] = table[...].T[0:rows].astype(jnp.bfloat16)


def entry_kernel(
    first_ref, fed_ref, handed_ref, gain_ref, routes_ref, gates_ref, entry_ref, sent_ref, table
):
    acts = jnp.where(first_ref[0] == 1, fed_ref[...], handed_ref[...])
    entry_ref[...] = acts
    send_rows(1, acts, gain_ref, routes_ref, gates_ref, sent_ref, table)


def start_kernel(acts_ref, gain_ref, routes_ref, gates_ref, sent_ref, table):
    send_rows(0, acts_ref[...], gain_ref, routes_ref, gates_ref, sent_ref, table)


def start(acts, gain, routes, gates):
    vmem = pl.BlockSpec(memory_space=pltpu.VMEM)
    rows, width = acts.shape
    return pl.pallas_call(
        start_kernel,
        out_shape=jax.ShapeDtypeStruct((rows, width + LANES), jnp.bfloat16),
        in_specs=[vmem] * 4,
        out_specs=vmem,
        scratch_shapes=[pltpu.VMEM((LANES, LANES), jnp.float32)],
        cost_estimate=pl.CostEstimate(
            flops=6 * acts.size, bytes_accessed=8 * acts.size, transcendentals=0
        ),
        name="start",
    )(acts, gain, routes, gates)


def part_kernel(down_ref, parted_ref, sems):
    part = parted_ref.shape[2]
    copies = [
        pltpu.make_async_copy(down_ref.at[:, pl.ds(i * part, part)], parted_ref.at[i], sems.at[i])
        for i in range(QUARTERS)
    ]
    for copy in copies:
        copy.start()
    for copy in copies:
        copy.wait()


def in_parts(down_w):
    rows, width = down_w.shape
    return pl.pallas_call(
        part_kernel,
        out_shape=jax.ShapeDtypeStruct((QUARTERS, rows, width // QUARTERS), jnp.bfloat16),
        in_specs=[pl.BlockSpec(memory_space=pltpu.HBM)],
        out_specs=pl.BlockSpec(memory_space=pltpu.VMEM),
        scratch_shapes=[pltpu.SemaphoreType.DMA((QUARTERS,))],
        cost_estimate=pl.CostEstimate(flops=0, bytes_accessed=4 * down_w.size, transcendentals=0),
        name="in_parts",
    )(down_w)


def enter(is_first, fed, handed, gain, routes, gates):
    vmem = pl.BlockSpec(memory_space=pltpu.VMEM)
    rows, width = fed.shape
    return pl.pallas_call(
        entry_kernel,
        out_shape=(
            jax.ShapeDtypeStruct((rows, width), jnp.bfloat16),
            jax.ShapeDtypeStruct((rows, width + LANES), jnp.bfloat16),
        ),
        in_specs=[pl.BlockSpec(memory_space=pltpu.SMEM)] + [vmem] * 5,
        out_specs=(vmem, vmem),
        scratch_shapes=[pltpu.VMEM((LANES, LANES), jnp.float32)],
        cost_estimate=pl.CostEstimate(flops=6 * fed.size, bytes_accessed=8 * fed.size, transcendentals=0),
        name="enter",
    )(is_first, fed, handed, gain, routes, gates)


def slot_tables(facts, wanted_ref, block_rows, capacity):
    rows = facts.shape[0]
    shape = (SUBLANES, LANES)
    which = lax.broadcasted_iota(jnp.int32, shape, 0)
    column = lax.broadcasted_iota(jnp.int32, shape, 1)
    same = (column < 8) & (
        ((which < 2) & (column == which))
        | ((which >= 2) & (which < 4) & (column >= 2) & (column % 2 == which % 2))
    )
    told = lax.dot_general(
        jnp.where(same, 1.0, 0.0).astype(jnp.bfloat16),
        facts,
        (((1,), (1,)), ((), ())),
        preferred_element_type=jnp.float32,
    )
    ahead = lax.broadcasted_iota(jnp.int32, (SUBLANES, rows), 0)
    wanted = jnp.full((SUBLANES, rows), -9, jnp.int32)
    for i in range(QUARTERS):
        wanted = jnp.where(ahead == i, wanted_ref[i], wanted)
    wanted = wanted.astype(jnp.float32)
    first = told[0:1, :] == wanted
    second = told[1:2, :] == wanted
    gate = jnp.where(first, told[2:3, :], 0.0) + jnp.where(second, told[3:4, :], 0.0)
    hit = first | second
    source = lax.broadcasted_iota(jnp.int32, (rows, rows), 0)
    target = lax.broadcasted_iota(jnp.int32, (rows, rows), 1)
    blocks = rows // block_rows
    start = jnp.zeros((1, rows), jnp.int32)
    lane = lax.broadcasted_iota(jnp.int32, (1, rows), 1)
    for i in range(1, blocks):
        start = jnp.where(lane >= i * block_rows, i * block_rows, start)
    earlier = (source < target) & (source >= start)
    position = jnp.dot(
        jnp.where(hit, 1.0, 0.0).astype(jnp.bfloat16),
        jnp.where(earlier, 1.0, 0.0).astype(jnp.bfloat16),
        preferred_element_type=jnp.float32,
    ).astype(jnp.int32)
    base = jnp.zeros((1, rows), jnp.int32)
    for i in range(1, blocks):
        base = jnp.where(lane >= i * block_rows, i * capacity, base)
    return (jnp.where(hit, base + position, -1), gate)


def up_kernel(
    capacity, block_rows, wanted_ref, tokens_ref, own_g, own_u, after_g, after_u, far_g, far_u,
    before_g, before_u, packed_ref, place_ref, gate_ref, tokens, weights, sems, token_sem,
):
    token_copy = pltpu.make_async_copy(tokens_ref, tokens, token_sem)
    token_copy.start()
    pieces = (own_g, own_u, after_g, after_u, far_g, far_u, before_g, before_u)
    copies = [pltpu.make_async_copy(pieces[i], weights.at[i], sems.at[i]) for i in range(2 * QUARTERS)]
    for copy in copies[:4]:
        copy.start()
    token_copy.wait()
    rows = tokens.shape[0]
    width = tokens.shape[1] - LANES
    slots = packed_ref.shape[1]
    place, gate = slot_tables(tokens[:, width:], wanted_ref, block_rows, capacity)
    place_ref[...] = place
    gate_ref[...] = gate
    slot = lax.broadcasted_iota(jnp.int32, (slots, rows), 0)
    pack = jnp.concatenate(
        [
            jnp.where(slot == place[ahead : ahead + 1, :], 1.0, 0.0).astype(jnp.bfloat16)
            for ahead in range(QUARTERS)
        ],
        axis=0,
    )
    sent = jnp.dot(pack, tokens[:, :width], preferred_element_type=jnp.float32).astype(jnp.bfloat16)
    for ahead in range(QUARTERS):
        copies[2 * ahead].wait()
        copies[2 * ahead + 1].wait()
        if ahead < 2:
            copies[2 * ahead + 4].start()
            copies[2 * ahead + 5].start()
        mine = sent[ahead * slots : (ahead + 1) * slots]
        both = jnp.concatenate([weights[2 * ahead], weights[2 * ahead + 1]], axis=1)
        inner = jnp.dot(
            mine[:, : width // 2], both[: width // 2], preferred_element_type=jnp.float32
        )
        inner = inner + jnp.dot(
            mine[:, width // 2 :], both[width // 2 :], preferred_element_type=jnp.float32
        )
        units = inner.shape[1] // 2
        gates = inner[:, :units]
        hidden = gates / (1.0 + jnp.exp(-gates)) * inner[:, units:]
        packed_ref[ahead] = hidden.astype(jnp.bfloat16)


def expert_up(tokens, wanted, in_w, slots, block_rows):
    rows = tokens.shape[0]
    width, units = in_w[0].shape
    capacity = slots * block_rows // rows
    in_hbm = pl.BlockSpec(memory_space=pltpu.HBM)
    vmem = pl.BlockSpec(memory_space=pltpu.VMEM)
    return pl.pallas_call(
        functools.partial(up_kernel, capacity, block_rows),
        out_shape=(
            jax.ShapeDtypeStruct((QUARTERS, slots, units), jnp.bfloat16),
            jax.ShapeDtypeStruct((SUBLANES, rows), jnp.int32),
            jax.ShapeDtypeStruct((SUBLANES, rows), jnp.float32),
        ),
        in_specs=[pl.BlockSpec(memory_space=pltpu.SMEM)] + [in_hbm] * 9,
        out_specs=(vmem, vmem, vmem),
        scratch_shapes=[
            pltpu.VMEM(tokens.shape, jnp.bfloat16),
            pltpu.VMEM((2 * QUARTERS, width, units), jnp.bfloat16),
            pltpu.SemaphoreType.DMA((2 * QUARTERS,)),
            pltpu.SemaphoreType.DMA,
        ],
        compiler_params=pltpu.CompilerParams(vmem_limit_bytes=60 * MIB),
        cost_estimate=pl.CostEstimate(
            flops=2 * QUARTERS * slots * width * (2 * units + rows),
            bytes_accessed=2 * width * (rows + 2 * QUARTERS * units),
            transcendentals=QUARTERS * slots * units,
        ),
        name="expert_up",
    )(wanted, tokens, *in_w)


def down_kernel(
    hidden_ref, own, after, far, before, place_ref, gate_ref, out_ref, weights, parts, sems
):
    copies = [
        pltpu.make_async_copy(piece, weights.at[ahead], sems.at[ahead])
        for ahead, piece in enumerate((own, after, far, before))
    ]
    for copy in copies:
        copy.start()
    rows = out_ref.shape[0]
    slots = hidden_ref.shape[2]
    slot = lax.broadcasted_iota(jnp.int32, (slots, rows), 0)
    pack = []
    for ahead in range(QUARTERS):
        copies[ahead].wait()
        units = jnp.concatenate([hidden_ref[b, ahead] for b in range(QUARTERS)], axis=1)
        out = jnp.dot(units, weights[ahead], preferred_element_type=jnp.float32)
        here = slot == place_ref[ahead : ahead + 1, :]
        gate = jnp.sum(jnp.where(here, gate_ref[ahead : ahead + 1, :], 0.0), axis=1, keepdims=True)
        out = out * gate
        high = out.astype(jnp.bfloat16)
        parts[0, pl.ds(ahead * slots, slots)] = high
        parts[1, pl.ds(ahead * slots, slots)] = (out - high.astype(jnp.float32)).astype(jnp.bfloat16)
        pack.append(jnp.where(here, 1.0, 0.0))
    unpack = jnp.concatenate(pack, axis=0).T.astype(jnp.bfloat16)
    mixed = jnp.dot(unpack, parts[0], preferred_element_type=jnp.float32)
    mixed = mixed + jnp.dot(unpack, parts[1], preferred_element_type=jnp.float32)
    out_ref[...] = mixed.astype(jnp.bfloat16)


def expert_down(hidden, out_w, place, gate):
    rows = place.shape[1]
    units, part = out_w[0].shape
    slots = hidden.shape[2]
    in_hbm = pl.BlockSpec(memory_space=pltpu.HBM)
    vmem = pl.BlockSpec(memory_space=pltpu.VMEM)
    return pl.pallas_call(
        down_kernel,
        out_shape=jax.ShapeDtypeStruct((rows, part), jnp.bfloat16),
        in_specs=[vmem] + [in_hbm] * 4 + [vmem] * 2,
        out_specs=vmem,
        scratch_shapes=[
            pltpu.VMEM((QUARTERS, units, part), jnp.bfloat16),
            pltpu.VMEM((2, QUARTERS * slots, part), jnp.bfloat16),
            pltpu.SemaphoreType.DMA((QUARTERS,)),
        ],
        compiler_params=pltpu.CompilerParams(vmem_limit_bytes=60 * MIB),
        cost_estimate=pl.CostEstimate(
            flops=2 * QUARTERS * slots * part * (units + 2 * rows),
            bytes_accessed=2 * QUARTERS * units * (part + slots),
            transcendentals=0,
        ),
        name="expert_down",
    )(hidden, *out_w, place, gate)


def leave_kernel(entry_ref, returned_ref, out_ref):
    part = returned_ref.shape[2]
    for b in range(QUARTERS):
        columns = pl.ds(b * part, part)
        total = entry_ref[:, columns].astype(jnp.float32)
        for q in range(returned_ref.shape[0] // QUARTERS):
            total = total + returned_ref[q * QUARTERS + b].astype(jnp.float32)
        out_ref[:, columns] = total.astype(jnp.bfloat16)


def leave(entry, returned):
    vmem = pl.BlockSpec(memory_space=pltpu.VMEM)
    return pl.pallas_call(
        leave_kernel,
        out_shape=jax.ShapeDtypeStruct(entry.shape, jnp.bfloat16),
        in_specs=[vmem] * 2,
        out_specs=vmem,
        cost_estimate=pl.CostEstimate(
            flops=returned.size, bytes_accessed=2 * returned.size + 4 * entry.size, transcendentals=0
        ),
        name="leave",
    )(entry, returned)


def layer(entry, sent, wanted, in_w, out_w, slots):
    rows, width = entry.shape
    tokens = lax.all_gather(sent, RING, tiled=True)
    hidden, place, gate = expert_up(tokens, wanted, in_w, slots, rows)
    hidden = lax.all_gather(hidden, "b", axis=0)
    mixed = expert_down(hidden, out_w, place, gate)
    returned = swap(mixed.reshape(-1, rows, width // QUARTERS), RING)
    return leave(entry, returned)


def on_device(hidden_in, incoming, routes, gates, norm_gain, w_gate, w_up, w_down):
    section_place = lax.axis_index("section")
    rows, width = incoming.shape
    n_store = lax.axis_size(STORE)
    experts = n_store // HS
    capacity = HS * ((rows * TOPK + experts * HS - 1) // (experts * HS))
    part = width // QUARTERS
    ring = lax.axis_size(RING)
    slots = ring * capacity
    routes, gates = [jnp.swapaxes(a[:, 0], 1, 2) for a in (routes, gates)]
    sent = start(hidden_in[0], norm_gain, routes, gates)
    parted = in_parts(w_down[0])

    gate_w, up_w = w_gate[0], w_up[0]
    after_gate = fetched(gate_w, "y", 1)
    before_up = fetched(up_w, "y", 3)
    after_up = fetched(up_w, "y", 1)
    before_gate = fetched(gate_w, "y", 3)
    far_up = fetched(after_up, "y", 1)
    far_gate = fetched(before_gate, "y", 3)
    in_w = (gate_w, up_w, after_gate, after_up, far_gate, far_up, before_gate, before_up)
    out_w = swap(parted, "b").reshape(-1, part)
    out_w, _, _ = lax.optimization_barrier((out_w, after_gate, before_up))
    out_w = (out_w,) + tuple(fetched(out_w, "y", ahead) for ahead in (1, 2, 3))
    ring_place = lax.axis_index(RING)
    y_place = (lax.axis_index("y") + jnp.arange(QUARTERS, dtype=jnp.int32)) % QUARTERS
    wanted = y_place * (ring // HS) + ring_place // HS
    first = layer(hidden_in[0], sent, wanted, in_w, out_w, slots)
    handed = shifted(first, "section", 1)
    is_first = (section_place == 0).astype(jnp.int32).reshape(1)
    entry, sent = enter(is_first, incoming, handed, norm_gain, routes, gates)
    second = layer(entry, sent, wanted, in_w, out_w, slots)
    return (first[None], second[None])


def solution(mesh):
    sections, stores = mesh.devices.shape
    fine = Mesh(
        mesh.devices.reshape(sections, 4, stores // (4 * QUARTERS), QUARTERS),
        ("section",) + STORE,
    )
    placed = (
        P("section", STORE, None),
        P(STORE, None),
        P(None, "section", STORE, None),
        P(None, "section", STORE, None),
        P("section", None),
        P("section", None, STORE),
        P("section", None, STORE),
        P("section", STORE, None),
    )
    return jax.shard_map(
        on_device,
        mesh=fine,
        in_specs=placed,
        out_specs=(P("section", STORE, None), P("section", STORE, None)),
        check_vma=False,
    )
```

```python
import functools

import jax
import jax.numpy as jnp
from jax import lax
from jax.experimental import pallas as pl
from jax.experimental.pallas import tpu as pltpu
from jax.sharding import Mesh, PartitionSpec as P

TOPK = 2
HS = 8
QUARTERS = 4


HIGH = lax.Precision.HIGHEST
RING = ("q", "b")
STORE = ("y",) + RING
MIB = 1 << 20
LANES = 128
SUBLANES = 8
CHUNKS = 7


def shifted(shard, axis, by):
    peers = lax.axis_size(axis)
    pairs = [(i, i + by) for i in range(peers) if 0 <= i + by < peers]
    return lax.ppermute(shard, axis, pairs)


def fetched(shard, axis, ahead):
    peers = lax.axis_size(axis)
    return lax.ppermute(shard, axis, [((i + ahead) % peers, i) for i in range(peers)])


def swap(blocks, axis):
    return lax.all_to_all(blocks, axis, split_axis=0, concat_axis=0, tiled=True)


def send_rows(tick, acts, gain_ref, routes_ref, gates_ref, sent_ref, table):
    rows, width = acts.shape
    values = acts.astype(jnp.float32)
    scale = lax.rsqrt(jnp.mean(values * values, axis=-1, keepdims=True) + 1e-06)
    sent_ref[:, :width] = (values * scale * gain_ref[...]).astype(jnp.bfloat16)
    gates = gates_ref[tick]
    high = gates.astype(jnp.bfloat16).astype(jnp.float32)
    middle = (gates - high).astype(jnp.bfloat16).astype(jnp.float32)
    table[...] = jnp.zeros_like(table)
    table[0:2, 0:rows] = routes_ref[tick].astype(jnp.float32)
    table[2:4, 0:rows] = high
    table[4:6, 0:rows] = middle
    table[6:8, 0:rows] = gates - high - middle
    sent_ref[:, width:] = table[...].T[0:rows].astype(jnp.bfloat16)


def entry_kernel(
    first_ref, fed_ref, handed_ref, gain_ref, routes_ref, gates_ref, entry_ref, sent_ref, table
):
    acts = jnp.where(first_ref[0] == 1, fed_ref[...], handed_ref[...])
    entry_ref[...] = acts
    send_rows(1, acts, gain_ref, routes_ref, gates_ref, sent_ref, table)


def start_kernel(acts_ref, gain_ref, routes_ref, gates_ref, sent_ref, table):
    send_rows(0, acts_ref[...], gain_ref, routes_ref, gates_ref, sent_ref, table)


def start(acts, gain, routes, gates):
    vmem = pl.BlockSpec(memory_space=pltpu.VMEM)
    rows, width = acts.shape
    return pl.pallas_call(
        start_kernel,
        out_shape=jax.ShapeDtypeStruct((rows, width + LANES), jnp.bfloat16),
        in_specs=[vmem] * 4,
        out_specs=vmem,
        scratch_shapes=[pltpu.VMEM((LANES, LANES), jnp.float32)],
        cost_estimate=pl.CostEstimate(
            flops=6 * acts.size, bytes_accessed=8 * acts.size, transcendentals=0
        ),
        name="start",
    )(acts, gain, routes, gates)


def part_kernel(down_ref, parted_ref, sems):
    part = parted_ref.shape[2]
    copies = [
        pltpu.make_async_copy(down_ref.at[:, pl.ds(i * part, part)], parted_ref.at[i], sems.at[i])
        for i in range(QUARTERS)
    ]
    for copy in copies:
        copy.start()
    for copy in copies:
        copy.wait()


def in_parts(down_w):
    rows, width = down_w.shape
    return pl.pallas_call(
        part_kernel,
        out_shape=jax.ShapeDtypeStruct((QUARTERS, rows, width // QUARTERS), jnp.bfloat16),
        in_specs=[pl.BlockSpec(memory_space=pltpu.HBM)],
        out_specs=pl.BlockSpec(memory_space=pltpu.VMEM),
        scratch_shapes=[pltpu.SemaphoreType.DMA((QUARTERS,))],
        cost_estimate=pl.CostEstimate(flops=0, bytes_accessed=4 * down_w.size, transcendentals=0),
        name="in_parts",
    )(down_w)


def enter(is_first, fed, handed, gain, routes, gates):
    vmem = pl.BlockSpec(memory_space=pltpu.VMEM)
    rows, width = fed.shape
    return pl.pallas_call(
        entry_kernel,
        out_shape=(
            jax.ShapeDtypeStruct((rows, width), jnp.bfloat16),
            jax.ShapeDtypeStruct((rows, width + LANES), jnp.bfloat16),
        ),
        in_specs=[pl.BlockSpec(memory_space=pltpu.SMEM)] + [vmem] * 5,
        out_specs=(vmem, vmem),
        scratch_shapes=[pltpu.VMEM((LANES, LANES), jnp.float32)],
        cost_estimate=pl.CostEstimate(flops=6 * fed.size, bytes_accessed=8 * fed.size, transcendentals=0),
        compiler_params=pltpu.CompilerParams(vmem_limit_bytes=8 * MIB),
        name="enter",
    )(is_first, fed, handed, gain, routes, gates)


def slot_tables(facts, wanted_ref, block_rows, capacity):
    rows = facts.shape[0]
    shape = (SUBLANES, LANES)
    which = lax.broadcasted_iota(jnp.int32, shape, 0)
    column = lax.broadcasted_iota(jnp.int32, shape, 1)
    same = (column < 8) & (
        ((which < 2) & (column == which))
        | ((which >= 2) & (which < 4) & (column >= 2) & (column % 2 == which % 2))
    )
    told = lax.dot_general(
        jnp.where(same, 1.0, 0.0).astype(jnp.bfloat16),
        facts,
        (((1,), (1,)), ((), ())),
        preferred_element_type=jnp.float32,
    )
    ahead = lax.broadcasted_iota(jnp.int32, (SUBLANES, rows), 0)
    wanted = jnp.full((SUBLANES, rows), -9, jnp.int32)
    for i in range(QUARTERS):
        wanted = jnp.where(ahead == i, wanted_ref[i], wanted)
    wanted = wanted.astype(jnp.float32)
    first = told[0:1, :] == wanted
    second = told[1:2, :] == wanted
    gate = jnp.where(first, told[2:3, :], 0.0) + jnp.where(second, told[3:4, :], 0.0)
    hit = first | second
    source = lax.broadcasted_iota(jnp.int32, (rows, rows), 0)
    target = lax.broadcasted_iota(jnp.int32, (rows, rows), 1)
    blocks = rows // block_rows
    start = jnp.zeros((1, rows), jnp.int32)
    lane = lax.broadcasted_iota(jnp.int32, (1, rows), 1)
    for i in range(1, blocks):
        start = jnp.where(lane >= i * block_rows, i * block_rows, start)
    earlier = (source < target) & (source >= start)
    position = jnp.dot(
        jnp.where(hit, 1.0, 0.0).astype(jnp.bfloat16),
        jnp.where(earlier, 1.0, 0.0).astype(jnp.bfloat16),
        preferred_element_type=jnp.float32,
    ).astype(jnp.int32)
    base = jnp.zeros((1, rows), jnp.int32)
    for i in range(1, blocks):
        base = jnp.where(lane >= i * block_rows, i * capacity, base)
    return (jnp.where(hit, base + position, -1), gate)


def up_kernel(
    capacity, block_rows, wanted_ref, tokens_ref, own_g, own_u, after_g, after_u, far_g, far_u,
    before_g, before_u, packed_ref, place_ref, gate_ref, tokens, facts, weights, total, sems, facts_sem,
):
    pieces = (own_g, own_u, after_g, after_u, far_g, far_u, before_g, before_u)
    rows, width = tokens.shape
    step = width // CHUNKS
    facts_copy = pltpu.make_async_copy(tokens_ref.at[:, pl.ds(width, LANES)], facts, facts_sem)
    facts_copy.start()
    copies = []
    for k in range(CHUNKS):
        part = pl.ds(k * step, step)
        group = [pltpu.make_async_copy(tokens_ref.at[:, part], tokens.at[:, part], sems.at[k, 2 * QUARTERS])]
        for i, piece in enumerate(pieces):
            group.append(pltpu.make_async_copy(piece.at[part], weights.at[i, part], sems.at[k, i]))
        for copy in group:
            copy.start()
        copies.append(group)
    slots, units = packed_ref.shape[1:]
    for k in range(CHUNKS):
        for copy in copies[k]:
            copy.wait()
        part = slice(k * step, (k + 1) * step)
        wide = jnp.concatenate([weights[i, part] for i in range(2 * QUARTERS)], axis=1)
        inner = jnp.dot(tokens[:, part], wide, preferred_element_type=jnp.float32)
        if k == 0:
            total[...] = inner
        else:
            total[...] += inner
    facts_copy.wait()
    place, gate = slot_tables(facts[...], wanted_ref, block_rows, capacity)
    place_ref[...] = place
    gate_ref[...] = gate
    slot = lax.broadcasted_iota(jnp.int32, (slots, rows), 0)
    for ahead in range(QUARTERS):
        first = 2 * ahead * units
        gates = total[:, first : first + units]
        hidden = gates / (1.0 + jnp.exp(-gates)) * total[:, first + units : first + 2 * units]
        pack = jnp.where(slot == place[ahead : ahead + 1, :], 1.0, 0.0).astype(jnp.bfloat16)
        packed = jnp.dot(pack, hidden.astype(jnp.bfloat16), preferred_element_type=jnp.float32)
        packed_ref[ahead] = packed.astype(jnp.bfloat16)


def expert_up(tokens, wanted, in_w, slots, block_rows):
    rows = tokens.shape[0]
    width, units = in_w[0].shape
    capacity = slots * block_rows // rows
    in_hbm = pl.BlockSpec(memory_space=pltpu.HBM)
    vmem = pl.BlockSpec(memory_space=pltpu.VMEM)
    return pl.pallas_call(
        functools.partial(up_kernel, capacity, block_rows),
        out_shape=(
            jax.ShapeDtypeStruct((QUARTERS, slots, units), jnp.bfloat16),
            jax.ShapeDtypeStruct((SUBLANES, rows), jnp.int32),
            jax.ShapeDtypeStruct((SUBLANES, rows), jnp.float32),
        ),
        in_specs=[pl.BlockSpec(memory_space=pltpu.SMEM)] + [in_hbm] * 9,
        out_specs=(vmem, vmem, vmem),
        scratch_shapes=[
            pltpu.VMEM((rows, width), jnp.bfloat16),
            pltpu.VMEM((rows, LANES), jnp.bfloat16),
            pltpu.VMEM((2 * QUARTERS, width, units), jnp.bfloat16),
            pltpu.VMEM((rows, 2 * QUARTERS * units), jnp.float32),
            pltpu.SemaphoreType.DMA((CHUNKS, 2 * QUARTERS + 1)),
            pltpu.SemaphoreType.DMA,
        ],
        compiler_params=pltpu.CompilerParams(vmem_limit_bytes=60 * MIB),
        cost_estimate=pl.CostEstimate(
            flops=4 * QUARTERS * rows * width * units,
            bytes_accessed=2 * width * (rows + 2 * QUARTERS * units),
            transcendentals=QUARTERS * rows * units,
        ),
        name="expert_up",
    )(wanted, tokens, *in_w)


def down_kernel(
    hidden_ref, own, after, far, before, place_ref, gate_ref, out_ref, weights, parts, sems
):
    copies = [
        pltpu.make_async_copy(piece, weights.at[ahead], sems.at[ahead])
        for ahead, piece in enumerate((own, after, far, before))
    ]
    for copy in copies:
        copy.start()
    rows = out_ref.shape[0]
    slots = hidden_ref.shape[2]
    slot = lax.broadcasted_iota(jnp.int32, (slots, rows), 0)
    pack = []
    for ahead in range(QUARTERS):
        copies[ahead].wait()
        units = jnp.concatenate([hidden_ref[b, ahead] for b in range(QUARTERS)], axis=1)
        out = jnp.dot(units, weights[ahead], preferred_element_type=jnp.float32)
        here = slot == place_ref[ahead : ahead + 1, :]
        gate = jnp.sum(jnp.where(here, gate_ref[ahead : ahead + 1, :], 0.0), axis=1, keepdims=True)
        out = out * gate
        high = out.astype(jnp.bfloat16)
        parts[0, pl.ds(ahead * slots, slots)] = high
        parts[1, pl.ds(ahead * slots, slots)] = (out - high.astype(jnp.float32)).astype(jnp.bfloat16)
        pack.append(jnp.where(here, 1.0, 0.0))
    unpack = jnp.concatenate(pack, axis=0).T.astype(jnp.bfloat16)
    mixed = jnp.dot(unpack, parts[0], preferred_element_type=jnp.float32)
    mixed = mixed + jnp.dot(unpack, parts[1], preferred_element_type=jnp.float32)
    out_ref[...] = mixed.astype(jnp.bfloat16)


def expert_down(hidden, out_w, place, gate):
    rows = place.shape[1]
    units, part = out_w[0].shape
    slots = hidden.shape[2]
    in_hbm = pl.BlockSpec(memory_space=pltpu.HBM)
    vmem = pl.BlockSpec(memory_space=pltpu.VMEM)
    return pl.pallas_call(
        down_kernel,
        out_shape=jax.ShapeDtypeStruct((rows, part), jnp.bfloat16),
        in_specs=[vmem] + [in_hbm] * 4 + [vmem] * 2,
        out_specs=vmem,
        scratch_shapes=[
            pltpu.VMEM((QUARTERS, units, part), jnp.bfloat16),
            pltpu.VMEM((2, QUARTERS * slots, part), jnp.bfloat16),
            pltpu.SemaphoreType.DMA((QUARTERS,)),
        ],
        compiler_params=pltpu.CompilerParams(vmem_limit_bytes=16 * MIB),
        cost_estimate=pl.CostEstimate(
            flops=2 * QUARTERS * slots * part * (units + 2 * rows),
            bytes_accessed=2 * QUARTERS * units * (part + slots),
            transcendentals=0,
        ),
        name="expert_down",
    )(hidden, *out_w, place, gate)


def leave_kernel(entry_ref, returned_ref, out_ref):
    part = returned_ref.shape[2]
    for b in range(QUARTERS):
        columns = pl.ds(b * part, part)
        total = entry_ref[:, columns].astype(jnp.float32)
        for q in range(returned_ref.shape[0] // QUARTERS):
            total = total + returned_ref[q * QUARTERS + b].astype(jnp.float32)
        out_ref[:, columns] = total.astype(jnp.bfloat16)


def leave(entry, returned):
    vmem = pl.BlockSpec(memory_space=pltpu.VMEM)
    return pl.pallas_call(
        leave_kernel,
        out_shape=jax.ShapeDtypeStruct(entry.shape, jnp.bfloat16),
        in_specs=[vmem] * 2,
        out_specs=vmem,
        cost_estimate=pl.CostEstimate(
            flops=returned.size, bytes_accessed=2 * returned.size + 4 * entry.size, transcendentals=0
        ),
        compiler_params=pltpu.CompilerParams(vmem_limit_bytes=8 * MIB),
        name="leave",
    )(entry, returned)


def layer(entry, sent, wanted, in_w, out_w, slots):
    rows, width = entry.shape
    tokens = lax.all_gather(sent, RING, tiled=True)
    hidden, place, gate = expert_up(tokens, wanted, in_w, slots, rows)
    hidden = lax.all_gather(hidden, "b", axis=0)
    mixed = expert_down(hidden, out_w, place, gate)
    returned = swap(mixed.reshape(-1, rows, width // QUARTERS), RING)
    return leave(entry, returned)


def on_device(hidden_in, incoming, routes, gates, norm_gain, w_gate, w_up, w_down):
    section_place = lax.axis_index("section")
    rows, width = incoming.shape
    n_store = lax.axis_size(STORE)
    experts = n_store // HS
    capacity = HS * ((rows * TOPK + experts * HS - 1) // (experts * HS))
    part = width // QUARTERS
    ring = lax.axis_size(RING)
    slots = ring * capacity
    routes, gates = [jnp.swapaxes(a[:, 0], 1, 2) for a in (routes, gates)]
    sent = start(hidden_in[0], norm_gain, routes, gates)
    parted = in_parts(w_down[0])

    gate_w, up_w = w_gate[0], w_up[0]
    after_gate = fetched(gate_w, "y", 1)
    before_up = fetched(up_w, "y", 3)
    after_up = fetched(up_w, "y", 1)
    before_gate = fetched(gate_w, "y", 3)
    far_up = fetched(after_up, "y", 1)
    far_gate = fetched(before_gate, "y", 3)
    in_w = (gate_w, up_w, after_gate, after_up, far_gate, far_up, before_gate, before_up)
    out_w = swap(parted, "b").reshape(-1, part)
    out_w, _, _ = lax.optimization_barrier((out_w, after_gate, before_up))
    out_w = (out_w,) + tuple(fetched(out_w, "y", ahead) for ahead in (1, 2, 3))
    ring_place = lax.axis_index(RING)
    y_place = (lax.axis_index("y") + jnp.arange(QUARTERS, dtype=jnp.int32)) % QUARTERS
    wanted = y_place * (ring // HS) + ring_place // HS
    first = layer(hidden_in[0], sent, wanted, in_w, out_w, slots)
    handed = shifted(first, "section", 1)
    is_first = (section_place == 0).astype(jnp.int32).reshape(1)
    entry, sent = enter(is_first, incoming, handed, norm_gain, routes, gates)
    second = layer(entry, sent, wanted, in_w, out_w, slots)
    return (first[None], second[None])


def solution(mesh):
    sections, stores = mesh.devices.shape
    fine = Mesh(
        mesh.devices.reshape(sections, 4, stores // (4 * QUARTERS), QUARTERS),
        ("section",) + STORE,
    )
    placed = (
        P("section", STORE, None),
        P(STORE, None),
        P(None, "section", STORE, None),
        P(None, "section", STORE, None),
        P("section", None),
        P("section", None, STORE),
        P("section", None, STORE),
        P("section", STORE, None),
    )
    return jax.shard_map(
        on_device,
        mesh=fine,
        in_specs=placed,
        out_specs=(P("section", STORE, None), P("section", STORE, None)),
        check_vma=False,
    )
```

```python
import functools

import jax
import jax.numpy as jnp
from jax import lax
from jax.experimental import pallas as pl
from jax.experimental.pallas import tpu as pltpu
from jax.sharding import Mesh, PartitionSpec as P

TOPK = 2
HS = 8
QUARTERS = 4


HIGH = lax.Precision.HIGHEST
RING = ("q", "b")
STORE = ("y",) + RING
MIB = 1 << 20
LANES = 128
SUBLANES = 8
CHUNKS = 7


def shifted(shard, axis, by):
    peers = lax.axis_size(axis)
    pairs = [(i, i + by) for i in range(peers) if 0 <= i + by < peers]
    return lax.ppermute(shard, axis, pairs)


def fetched(shard, axis, ahead):
    peers = lax.axis_size(axis)
    return lax.ppermute(shard, axis, [((i + ahead) % peers, i) for i in range(peers)])


def swap(blocks, axis):
    return lax.all_to_all(blocks, axis, split_axis=0, concat_axis=0, tiled=True)


def send_rows(tick, acts, gain_ref, routes_ref, gates_ref, sent_ref, table):
    rows, width = acts.shape
    values = acts.astype(jnp.float32)
    scale = lax.rsqrt(jnp.mean(values * values, axis=-1, keepdims=True) + 1e-06)
    sent_ref[:, :width] = (values * scale * gain_ref[...]).astype(jnp.bfloat16)
    gates = gates_ref[tick]
    high = gates.astype(jnp.bfloat16).astype(jnp.float32)
    middle = (gates - high).astype(jnp.bfloat16).astype(jnp.float32)
    table[...] = jnp.zeros_like(table)
    table[0:2, 0:rows] = routes_ref[tick].astype(jnp.float32)
    table[2:4, 0:rows] = high
    table[4:6, 0:rows] = middle
    table[6:8, 0:rows] = gates - high - middle
    sent_ref[:, width:] = table[...].T[0:rows].astype(jnp.bfloat16)


def entry_kernel(
    first_ref, fed_ref, handed_ref, gain_ref, routes_ref, gates_ref, entry_ref, sent_ref, table
):
    acts = jnp.where(first_ref[0] == 1, fed_ref[...], handed_ref[...])
    entry_ref[...] = acts
    send_rows(1, acts, gain_ref, routes_ref, gates_ref, sent_ref, table)


def start_kernel(acts_ref, gain_ref, routes_ref, gates_ref, sent_ref, table):
    send_rows(0, acts_ref[...], gain_ref, routes_ref, gates_ref, sent_ref, table)


def start(acts, gain, routes, gates):
    vmem = pl.BlockSpec(memory_space=pltpu.VMEM)
    rows, width = acts.shape
    return pl.pallas_call(
        start_kernel,
        out_shape=jax.ShapeDtypeStruct((rows, width + LANES), jnp.bfloat16),
        in_specs=[vmem] * 4,
        out_specs=vmem,
        scratch_shapes=[pltpu.VMEM((LANES, LANES), jnp.float32)],
        cost_estimate=pl.CostEstimate(
            flops=6 * acts.size, bytes_accessed=8 * acts.size, transcendentals=0
        ),
        name="start",
    )(acts, gain, routes, gates)


def part_kernel(down_ref, parted_ref, sems):
    part = parted_ref.shape[2]
    copies = [
        pltpu.make_async_copy(down_ref.at[:, pl.ds(i * part, part)], parted_ref.at[i], sems.at[i])
        for i in range(QUARTERS)
    ]
    for copy in copies:
        copy.start()
    for copy in copies:
        copy.wait()


def in_parts(down_w):
    rows, width = down_w.shape
    return pl.pallas_call(
        part_kernel,
        out_shape=jax.ShapeDtypeStruct((QUARTERS, rows, width // QUARTERS), jnp.bfloat16),
        in_specs=[pl.BlockSpec(memory_space=pltpu.HBM)],
        out_specs=pl.BlockSpec(memory_space=pltpu.VMEM),
        scratch_shapes=[pltpu.SemaphoreType.DMA((QUARTERS,))],
        cost_estimate=pl.CostEstimate(flops=0, bytes_accessed=4 * down_w.size, transcendentals=0),
        name="in_parts",
    )(down_w)


def enter(is_first, fed, handed, gain, routes, gates):
    vmem = pl.BlockSpec(memory_space=pltpu.VMEM)
    rows, width = fed.shape
    return pl.pallas_call(
        entry_kernel,
        out_shape=(
            jax.ShapeDtypeStruct((rows, width), jnp.bfloat16),
            jax.ShapeDtypeStruct((rows, width + LANES), jnp.bfloat16),
        ),
        in_specs=[pl.BlockSpec(memory_space=pltpu.SMEM)] + [vmem] * 5,
        out_specs=(vmem, vmem),
        scratch_shapes=[pltpu.VMEM((LANES, LANES), jnp.float32)],
        cost_estimate=pl.CostEstimate(flops=6 * fed.size, bytes_accessed=8 * fed.size, transcendentals=0),
        compiler_params=pltpu.CompilerParams(vmem_limit_bytes=8 * MIB),
        name="enter",
    )(is_first, fed, handed, gain, routes, gates)


def slot_tables(facts, wanted_ref, block_rows, capacity):
    rows = facts.shape[0]
    shape = (SUBLANES, LANES)
    which = lax.broadcasted_iota(jnp.int32, shape, 0)
    column = lax.broadcasted_iota(jnp.int32, shape, 1)
    same = (column < 8) & (
        ((which < 2) & (column == which))
        | ((which >= 2) & (which < 4) & (column >= 2) & (column % 2 == which % 2))
    )
    told = lax.dot_general(
        jnp.where(same, 1.0, 0.0).astype(jnp.bfloat16),
        facts,
        (((1,), (1,)), ((), ())),
        preferred_element_type=jnp.float32,
    )
    ahead = lax.broadcasted_iota(jnp.int32, (SUBLANES, rows), 0)
    wanted = jnp.full((SUBLANES, rows), -9, jnp.int32)
    for i in range(QUARTERS):
        wanted = jnp.where(ahead == i, wanted_ref[i], wanted)
    wanted = wanted.astype(jnp.float32)
    first = told[0:1, :] == wanted
    second = told[1:2, :] == wanted
    gate = jnp.where(first, told[2:3, :], 0.0) + jnp.where(second, told[3:4, :], 0.0)
    hit = first | second
    source = lax.broadcasted_iota(jnp.int32, (rows, rows), 0)
    target = lax.broadcasted_iota(jnp.int32, (rows, rows), 1)
    blocks = rows // block_rows
    start = jnp.zeros((1, rows), jnp.int32)
    lane = lax.broadcasted_iota(jnp.int32, (1, rows), 1)
    for i in range(1, blocks):
        start = jnp.where(lane >= i * block_rows, i * block_rows, start)
    earlier = (source < target) & (source >= start)
    position = jnp.dot(
        jnp.where(hit, 1.0, 0.0).astype(jnp.bfloat16),
        jnp.where(earlier, 1.0, 0.0).astype(jnp.bfloat16),
        preferred_element_type=jnp.float32,
    ).astype(jnp.int32)
    base = jnp.zeros((1, rows), jnp.int32)
    for i in range(1, blocks):
        base = jnp.where(lane >= i * block_rows, i * capacity, base)
    return (jnp.where(hit, base + position, -1), gate)


def up_kernel(
    capacity, block_rows, wanted_ref, tokens_ref, own_g, own_u, after_g, after_u, far_g, far_u,
    before_g, before_u, packed_ref, place_ref, gate_ref, tokens, facts, weights, total, sems, facts_sem,
):
    pieces = (own_g, own_u, after_g, after_u, far_g, far_u, before_g, before_u)
    rows, width = tokens.shape
    step = width // CHUNKS
    facts_copy = pltpu.make_async_copy(tokens_ref.at[:, pl.ds(width, LANES)], facts, facts_sem)
    facts_copy.start()
    copies = []
    for k in range(CHUNKS):
        part = pl.ds(k * step, step)
        group = [pltpu.make_async_copy(tokens_ref.at[:, part], tokens.at[:, part], sems.at[k, 2 * QUARTERS])]
        for i, piece in enumerate(pieces):
            group.append(pltpu.make_async_copy(piece.at[part], weights.at[i, part], sems.at[k, i]))
        for copy in group:
            copy.start()
        copies.append(group)
    slots, units = packed_ref.shape[1:]
    for k in range(CHUNKS):
        for copy in copies[k]:
            copy.wait()
        part = slice(k * step, (k + 1) * step)
        wide = jnp.concatenate([weights[i, part] for i in range(2 * QUARTERS)], axis=1)
        inner = jnp.dot(tokens[:, part], wide, preferred_element_type=jnp.float32)
        if k == 0:
            total[...] = inner
        else:
            total[...] += inner
    facts_copy.wait()
    place, gate = slot_tables(facts[...], wanted_ref, block_rows, capacity)
    place_ref[...] = place
    gate_ref[...] = gate
    slot = lax.broadcasted_iota(jnp.int32, (slots, rows), 0)
    for ahead in range(QUARTERS):
        first = 2 * ahead * units
        gates = total[:, first : first + units]
        hidden = gates / (1.0 + jnp.exp(-gates)) * total[:, first + units : first + 2 * units]
        pack = jnp.where(slot == place[ahead : ahead + 1, :], 1.0, 0.0).astype(jnp.bfloat16)
        packed = jnp.dot(pack, hidden.astype(jnp.bfloat16), preferred_element_type=jnp.float32)
        packed_ref[ahead] = packed.astype(jnp.bfloat16)


def expert_up(tokens, wanted, in_w, slots, block_rows):
    rows = tokens.shape[0]
    width, units = in_w[0].shape
    capacity = slots * block_rows // rows
    in_hbm = pl.BlockSpec(memory_space=pltpu.HBM)
    vmem = pl.BlockSpec(memory_space=pltpu.VMEM)
    return pl.pallas_call(
        functools.partial(up_kernel, capacity, block_rows),
        out_shape=(
            jax.ShapeDtypeStruct((QUARTERS, slots, units), jnp.bfloat16),
            jax.ShapeDtypeStruct((SUBLANES, rows), jnp.int32),
            jax.ShapeDtypeStruct((SUBLANES, rows), jnp.float32),
        ),
        in_specs=[pl.BlockSpec(memory_space=pltpu.SMEM)] + [in_hbm] * 9,
        out_specs=(vmem, vmem, vmem),
        scratch_shapes=[
            pltpu.VMEM((rows, width), jnp.bfloat16),
            pltpu.VMEM((rows, LANES), jnp.bfloat16),
            pltpu.VMEM((2 * QUARTERS, width, units), jnp.bfloat16),
            pltpu.VMEM((rows, 2 * QUARTERS * units), jnp.float32),
            pltpu.SemaphoreType.DMA((CHUNKS, 2 * QUARTERS + 1)),
            pltpu.SemaphoreType.DMA,
        ],
        compiler_params=pltpu.CompilerParams(vmem_limit_bytes=60 * MIB),
        cost_estimate=pl.CostEstimate(
            flops=4 * QUARTERS * rows * width * units,
            bytes_accessed=2 * width * (rows + 2 * QUARTERS * units),
            transcendentals=QUARTERS * rows * units,
        ),
        name="expert_up",
    )(wanted, tokens, *in_w)


def down_kernel(
    hidden_ref, own, after, far, before, place_ref, gate_ref, out_ref, weights, parts, sems
):
    copies = [
        pltpu.make_async_copy(piece, weights.at[ahead], sems.at[ahead])
        for ahead, piece in enumerate((own, after, far, before))
    ]
    for copy in copies:
        copy.start()
    rows = out_ref.shape[0]
    slots = hidden_ref.shape[2]
    slot = lax.broadcasted_iota(jnp.int32, (slots, rows), 0)
    pack = []
    for ahead in range(QUARTERS):
        copies[ahead].wait()
        units = jnp.concatenate([hidden_ref[b, ahead] for b in range(QUARTERS)], axis=1)
        out = jnp.dot(units, weights[ahead], preferred_element_type=jnp.float32)
        here = slot == place_ref[ahead : ahead + 1, :]
        gate = jnp.sum(jnp.where(here, gate_ref[ahead : ahead + 1, :], 0.0), axis=1, keepdims=True)
        out = out * gate
        high = out.astype(jnp.bfloat16)
        parts[0, pl.ds(ahead * slots, slots)] = high
        parts[1, pl.ds(ahead * slots, slots)] = (out - high.astype(jnp.float32)).astype(jnp.bfloat16)
        pack.append(jnp.where(here, 1.0, 0.0))
    unpack = jnp.concatenate(pack, axis=0).T.astype(jnp.bfloat16)
    mixed = jnp.dot(unpack, parts[0], preferred_element_type=jnp.float32)
    mixed = mixed + jnp.dot(unpack, parts[1], preferred_element_type=jnp.float32)
    out_ref[...] = mixed.astype(jnp.bfloat16)


def expert_down(hidden, out_w, place, gate):
    rows = place.shape[1]
    units, part = out_w[0].shape
    slots = hidden.shape[2]
    in_hbm = pl.BlockSpec(memory_space=pltpu.HBM)
    vmem = pl.BlockSpec(memory_space=pltpu.VMEM)
    return pl.pallas_call(
        down_kernel,
        out_shape=jax.ShapeDtypeStruct((rows, part), jnp.bfloat16),
        in_specs=[vmem] + [in_hbm] * 4 + [vmem] * 2,
        out_specs=vmem,
        scratch_shapes=[
            pltpu.VMEM((QUARTERS, units, part), jnp.bfloat16),
            pltpu.VMEM((2, QUARTERS * slots, part), jnp.bfloat16),
            pltpu.SemaphoreType.DMA((QUARTERS,)),
        ],
        compiler_params=pltpu.CompilerParams(vmem_limit_bytes=16 * MIB),
        cost_estimate=pl.CostEstimate(
            flops=2 * QUARTERS * slots * part * (units + 2 * rows),
            bytes_accessed=2 * QUARTERS * units * (part + slots),
            transcendentals=0,
        ),
        name="expert_down",
    )(hidden, *out_w, place, gate)


def leave_kernel(entry_ref, returned_ref, out_ref):
    part = returned_ref.shape[2]
    for b in range(QUARTERS):
        columns = pl.ds(b * part, part)
        total = entry_ref[:, columns].astype(jnp.float32)
        for q in range(returned_ref.shape[0] // QUARTERS):
            total = total + returned_ref[q * QUARTERS + b].astype(jnp.float32)
        out_ref[:, columns] = total.astype(jnp.bfloat16)


def leave(entry, returned):
    vmem = pl.BlockSpec(memory_space=pltpu.VMEM)
    return pl.pallas_call(
        leave_kernel,
        out_shape=jax.ShapeDtypeStruct(entry.shape, jnp.bfloat16),
        in_specs=[vmem] * 2,
        out_specs=vmem,
        cost_estimate=pl.CostEstimate(
            flops=returned.size, bytes_accessed=2 * returned.size + 4 * entry.size, transcendentals=0
        ),
        compiler_params=pltpu.CompilerParams(vmem_limit_bytes=8 * MIB),
        name="leave",
    )(entry, returned)


def layer(entry, sent, wanted, in_w, out_w, slots):
    rows, width = entry.shape
    tokens = lax.all_gather(sent, RING, tiled=True)
    hidden, place, gate = expert_up(tokens, wanted, in_w, slots, rows)
    hidden = lax.all_gather(hidden, "b", axis=0)
    mixed = expert_down(hidden, out_w, place, gate)
    returned = swap(mixed.reshape(-1, rows, width // QUARTERS), RING)
    return leave(entry, returned)


def on_device(hidden_in, incoming, routes, gates, norm_gain, w_gate, w_up, w_down):
    section_place = lax.axis_index("section")
    rows, width = incoming.shape
    n_store = lax.axis_size(STORE)
    experts = n_store // HS
    capacity = HS * ((rows * TOPK + experts * HS - 1) // (experts * HS))
    part = width // QUARTERS
    ring = lax.axis_size(RING)
    slots = ring * capacity
    routes, gates = [jnp.swapaxes(a[:, 0], 1, 2) for a in (routes, gates)]
    sent = start(hidden_in[0], norm_gain, routes, gates)
    parted = in_parts(w_down[0])

    gate_w, up_w = w_gate[0], w_up[0]
    after_gate = fetched(gate_w, "y", 1)
    before_up = fetched(up_w, "y", 3)
    after_up = fetched(up_w, "y", 1)
    before_gate = fetched(gate_w, "y", 3)
    far_up = fetched(after_up, "y", 1)
    far_gate = fetched(before_gate, "y", 3)
    in_w = (gate_w, up_w, after_gate, after_up, far_gate, far_up, before_gate, before_up)
    out_w = swap(parted, "b").reshape(-1, part)
    out_w, _, _ = lax.optimization_barrier((out_w, after_gate, before_up))
    out_after, out_before = fetched(out_w, "y", 1), fetched(out_w, "y", 3)
    far_w, far_gate, far_up = lax.optimization_barrier((out_w, far_gate, far_up))
    in_w = (gate_w, up_w, after_gate, after_up, far_gate, far_up, before_gate, before_up)
    out_w = (out_w, out_after, fetched(far_w, "y", 2), out_before)
    ring_place = lax.axis_index(RING)
    y_place = (lax.axis_index("y") + jnp.arange(QUARTERS, dtype=jnp.int32)) % QUARTERS
    wanted = y_place * (ring // HS) + ring_place // HS
    first = layer(hidden_in[0], sent, wanted, in_w, out_w, slots)
    handed = shifted(first, "section", 1)
    is_first = (section_place == 0).astype(jnp.int32).reshape(1)
    entry, sent = enter(is_first, incoming, handed, norm_gain, routes, gates)
    second = layer(entry, sent, wanted, in_w, out_w, slots)
    return (first[None], second[None])


def solution(mesh):
    sections, stores = mesh.devices.shape
    fine = Mesh(
        mesh.devices.reshape(sections, 4, stores // (4 * QUARTERS), QUARTERS),
        ("section",) + STORE,
    )
    placed = (
        P("section", STORE, None),
        P(STORE, None),
        P(None, "section", STORE, None),
        P(None, "section", STORE, None),
        P("section", None),
        P("section", None, STORE),
        P("section", None, STORE),
        P("section", STORE, None),
    )
    return jax.shard_map(
        on_device,
        mesh=fine,
        in_specs=placed,
        out_specs=(P("section", STORE, None), P("section", STORE, None)),
        check_vma=False,
    )
```
